32 devices in a mesh: lat: 4 (over y, core), lon: 8 (over z, x).
Axes of the slice: x: 2, y: 2, z: 4, core: 2. Of those that a mesh axis runs over, the one named last changes fastest.
Arguments:
- latent: bfloat16 [64, 768, 256], P('lat', 'lon'), may hold values from -6 to 6
- ocean_mask: int32 [64, 768], P('lat', 'lon'), may hold values from 0 to 1, as said below
- depth_kernel: bfloat16 [7, 7, 256], replicated, may hold values from -0.875 to 0.875
- expand_weight: bfloat16 [256, 1024], replicated, may hold values from -0.375 to 0.375
- reduce_weight: bfloat16 [1024, 256], replicated, may hold values from -0.1875 to 0.1875
- decode_weight: bfloat16 [256, 304], replicated, may hold values from -0.375 to 0.375
- column_in: bfloat16 [304, 1024], replicated, may hold values from -0.3125 to 0.3125
- column_out: bfloat16 [1024, 304], replicated, may hold values from -0.1875 to 0.1875
- state_cot: bfloat16 [64, 768, 304], P('lat', 'lon'), may hold values from -6 to 6
Outputs:
- state: bfloat16 [64, 768, 304], P('lat', 'lon')
- grad_latent: bfloat16 [64, 768, 256], P('lat', 'lon')
- grad_kernel: float32 [7, 7, 256], P(None, None, ('lat', 'lon'))
- grad_expand: float32 [256, 1024], P(None, ('lat', 'lon'))
- grad_reduce: float32 [1024, 256], P(('lat', 'lon'))
- grad_decode: float32 [256, 304], P(('lat', 'lon'))
- grad_column_in: float32 [304, 1024], P(None, ('lat', 'lon'))
- grad_column_out: float32 [1024, 304], P(('lat', 'lon'))
The draws below stay inside these ranges and needn't reach their ends.
Inputs may be any that keep to these rules, and one draw needn't show every extreme that they name: `ocean_mask`: exactly 18432 cells are ocean (1), the rest land (0); at least one device's tile is all ocean.
All inputs are finite; a program needn't handle non-finite values.
Results may differ from the reference program's by a relative error of at most 0.008.
Values may be sent and summed in bfloat16 or wider, within the bound.
A program may use at most 128 MiB of HBM per device.

```python
import math
import jax
import jax.numpy as jnp
from jax import lax

C = 256
EXPAND = 1024
COLVALS = 304
COLHID = 1024
KERNEL = 7
HL = 16
WL = 96
NLAT = 64
NLON = 768
OCEAN = 18432


def draw_ocean_mask(key, part):
    tile_key, full_key, cell_key, order_key = jax.random.split(key, 4)
    tiles_lat = NLAT // HL
    tiles_lon = NLON // WL
    tile_total = tiles_lat * tiles_lon
    levels = jax.random.randint(tile_key, (tile_total,), 0, 6)
    full_tile = jax.random.randint(full_key, (), 0, tile_total)
    levels = jnp.where(jnp.arange(tile_total) == full_tile, -4, levels)
    lat_ids = jnp.arange(NLAT) // HL
    lon_ids = jnp.arange(NLON) // WL
    tile_ids = (lat_ids[:, None] * tiles_lon + lon_ids[None, :]).reshape(-1)
    scores = levels[tile_ids] + jax.random.randint(cell_key, (NLAT * NLON,), 0, 4)
    shuffled = jax.random.permutation(order_key, NLAT * NLON)
    ordering = shuffled[jnp.argsort(scores[shuffled], stable=True)]
    rank_of = jnp.zeros((NLAT * NLON,), jnp.int32).at[ordering].set(jnp.arange(NLAT * NLON, dtype=jnp.int32))
    return (rank_of < OCEAN).astype(jnp.int32).reshape(NLAT, NLON)


def block_levels(stream_key, shape, pieces, smallest, high):
    level = 1.0
    for axis_at, parts in pieces:
        heights = jax.random.uniform(jax.random.fold_in(jax.random.fold_in(stream_key, 6), axis_at), (parts,), jnp.float32, smallest / len(pieces), high / len(pieces))
        level = level * jnp.repeat(jnp.exp(heights), shape[axis_at] // parts).reshape((-1,) + (1,) * (len(shape) - 1 - axis_at))
    return level


def bell_draw(rng, shape, scale, bound, cuts=(), held_as=jnp.bfloat16):
    level = block_levels(rng, shape, cuts, -0.22, 0.18) if cuts else 1.0
    entries = jax.random.normal(rng, shape, jnp.float32) * scale * level
    return jnp.minimum(jnp.maximum(entries, -bound), bound).astype(held_as)


def setup_inputs(seed: int = 0) -> dict:
    splits = jax.random.split(jax.random.key(seed), 10)
    return {
        "latent": bell_draw(splits[0], (NLAT, NLON, C), 1.0, 6.0, ((0, 4), (1, 8))),
        "ocean_mask": draw_ocean_mask(jax.random.fold_in(splits[9], 71), 0),
        "depth_kernel": bell_draw(splits[2], (KERNEL, KERNEL, C), (KERNEL * KERNEL) ** -0.5, 0.875),
        "expand_weight": bell_draw(splits[3], (C, EXPAND), C ** -0.5, 0.375),
        "reduce_weight": bell_draw(splits[4], (EXPAND, C), EXPAND ** -0.5, 0.1875),
        "decode_weight": bell_draw(splits[5], (C, COLVALS), C ** -0.5, 0.375),
        "column_in": bell_draw(splits[6], (COLVALS, COLHID), COLVALS ** -0.5, 0.3125),
        "column_out": bell_draw(splits[7], (COLHID, COLVALS), COLHID ** -0.5, 0.1875),
        "state_cot": bell_draw(splits[8], (NLAT, NLON, COLVALS), 1.0, 6.0, ((0, 4), (1, 8))),
    }


EPSILON = 1e-06

def gelu_fn(values_in):
    return jax.nn.gelu(values_in, approximate=True)

def gelu_back(pre_act, upstream):
    return jax.vjp(gelu_fn, pre_act)[1](upstream)[0]

def pad_grid(grid_field):
    radius_cells = KERNEL // 2
    wrapped = jnp.concatenate([grid_field[:, -radius_cells:], grid_field, grid_field[:, :radius_cells]], axis=1)
    return jnp.pad(wrapped, ((radius_cells, radius_cells), (0, 0), (0, 0)))

def depthwise(padded, kernel, row_count, col_count):
    summed = jnp.zeros((row_count, col_count, padded.shape[2]), jnp.float32)
    for row_off in range(kernel.shape[0]):
        for col_off in range(kernel.shape[1]):
            window = padded[row_off:row_off + row_count, col_off:col_off + col_count].astype(jnp.float32)
            summed = summed + kernel[row_off, col_off].astype(jnp.float32) * window
    return summed

def back_conv(wide_grad, kernel, row_count, col_count):
    kernel_span = kernel.shape[0] - 1
    summed = jnp.zeros((row_count, col_count, wide_grad.shape[2]), jnp.float32)
    for row_off in range(kernel.shape[0]):
        for col_off in range(kernel.shape[1]):
            low_row = kernel_span - row_off
            low_col = kernel_span - col_off
            window = wide_grad[low_row:low_row + row_count, low_col:low_col + col_count].astype(jnp.float32)
            summed = summed + kernel[row_off, col_off].astype(jnp.float32) * window
    return summed

def kernel_terms(wide_field, grad_field, kernel_size):
    row_count = grad_field.shape[0]
    col_count = grad_field.shape[1]
    terms_list = []
    for row_off in range(kernel_size):
        for col_off in range(kernel_size):
            window = wide_field[row_off:row_off + row_count, col_off:col_off + col_count].astype(jnp.float32)
            terms_list.append(lax.optimization_barrier(jnp.sum(grad_field * window, axis=(0, 1))))
    return jnp.stack(terms_list).reshape(kernel_size, kernel_size, grad_field.shape[2])

def reference(latent, ocean_mask, depth_kernel, expand_weight, reduce_weight, decode_weight, column_in, column_out, state_cot):
    ocean = ocean_mask.astype(latent.dtype)
    masked = latent * ocean[:, :, None]
    padded = pad_grid(masked)
    convolved = depthwise(padded, depth_kernel, NLAT, NLON)
    block_total = NLAT // HL
    block_cells = HL * NLON
    conv_blocks = convolved.reshape(block_total, block_cells, C)
    masked_blocks = masked.reshape(block_total, block_cells, C)
    ocean_blocks = ocean_mask.reshape(block_total, block_cells)
    cot_blocks = state_cot.reshape(block_total, block_cells, COLVALS)

    def block_step(carry, block_data):
        conv_rows, masked_rows, ocean_rows, cot_rows = block_data
        row_mean = lax.optimization_barrier(jnp.mean(conv_rows, axis=1, keepdims=True))
        centred = conv_rows - row_mean
        inverse_scale = lax.rsqrt(lax.optimization_barrier(jnp.mean(centred * centred, axis=1, keepdims=True)) + EPSILON)
        unit_rows = centred * inverse_scale
        normed = unit_rows.astype(jnp.bfloat16)
        expand_pre = jnp.dot(normed, expand_weight, preferred_element_type=jnp.float32)
        hidden = gelu_fn(expand_pre).astype(jnp.bfloat16)
        feature = (masked_rows.astype(jnp.float32) + jnp.dot(hidden, reduce_weight, preferred_element_type=jnp.float32)).astype(jnp.bfloat16)
        column = jnp.dot(feature, decode_weight, preferred_element_type=jnp.float32).astype(jnp.bfloat16)
        column_pre = jnp.dot(column, column_in, preferred_element_type=jnp.float32)
        inner = gelu_fn(column_pre).astype(jnp.bfloat16)
        ocean_col = ocean_rows.astype(jnp.float32)[:, None]
        state_rows = (ocean_col * (column.astype(jnp.float32) + jnp.dot(inner, column_out, preferred_element_type=jnp.float32))).astype(jnp.bfloat16)
        target = (cot_rows.astype(jnp.float32) * ocean_col).astype(jnp.bfloat16)
        inner_back = jnp.dot(target, column_out.T, preferred_element_type=jnp.float32)
        column_pre_grad = gelu_back(column_pre, inner_back).astype(jnp.bfloat16)
        column_grad = (target.astype(jnp.float32) + jnp.dot(column_pre_grad, column_in.T, preferred_element_type=jnp.float32)).astype(jnp.bfloat16)
        feature_back = jnp.dot(column_grad, decode_weight.T, preferred_element_type=jnp.float32)
        feature_grad = feature_back.astype(jnp.bfloat16)
        hidden_back = jnp.dot(feature_grad, reduce_weight.T, preferred_element_type=jnp.float32)
        expand_grad = gelu_back(expand_pre, hidden_back).astype(jnp.bfloat16)
        normed_back = jnp.dot(expand_grad, expand_weight.T, preferred_element_type=jnp.float32)
        conv_grad = (inverse_scale * (normed_back - lax.optimization_barrier(jnp.mean(normed_back, axis=1, keepdims=True)) - unit_rows * lax.optimization_barrier(jnp.mean(normed_back * unit_rows, axis=1, keepdims=True)))).astype(jnp.bfloat16)
        grad_expand, grad_reduce, grad_decode, grad_cin, grad_cout = carry
        grad_expand = grad_expand + jnp.dot(normed.T, expand_grad, preferred_element_type=jnp.float32)
        grad_reduce = grad_reduce + jnp.dot(hidden.T, feature_grad, preferred_element_type=jnp.float32)
        grad_decode = grad_decode + jnp.dot(feature.T, column_grad, preferred_element_type=jnp.float32)
        grad_cin = grad_cin + jnp.dot(column.T, column_pre_grad, preferred_element_type=jnp.float32)
        grad_cout = grad_cout + jnp.dot(inner.T, target, preferred_element_type=jnp.float32)
        return ((grad_expand, grad_reduce, grad_decode, grad_cin, grad_cout), (state_rows, conv_grad, feature_back))
    start_grads = (jnp.zeros((C, EXPAND), jnp.float32), jnp.zeros((EXPAND, C), jnp.float32), jnp.zeros((C, COLVALS), jnp.float32), jnp.zeros((COLVALS, COLHID), jnp.float32), jnp.zeros((COLHID, COLVALS), jnp.float32))
    final_grads, block_outs = lax.scan(block_step, start_grads, (conv_blocks, masked_blocks, ocean_blocks, cot_blocks))
    state_blocks, conv_grad_blocks, feature_blocks = block_outs
    state = state_blocks.reshape(NLAT, NLON, COLVALS)
    conv_grad = conv_grad_blocks.reshape(NLAT, NLON, C)
    feature_back = feature_blocks.reshape(NLAT, NLON, C)
    wide_grad = pad_grid(conv_grad)
    grad_kernel = kernel_terms(padded, conv_grad.astype(jnp.float32), KERNEL)
    back_terms = back_conv(wide_grad, depth_kernel, NLAT, NLON)
    grad_latent = (ocean_mask.astype(jnp.float32)[:, :, None] * (feature_back + back_terms)).astype(jnp.bfloat16)
    grad_scale = 1.0 / math.sqrt(NLAT * NLON)
    grad_expand, grad_reduce, grad_decode, grad_cin, grad_cout = final_grads
    return (state, grad_latent, grad_kernel * grad_scale, grad_expand * grad_scale, grad_reduce * grad_scale, grad_decode * grad_scale, grad_cin * grad_scale, grad_cout * grad_scale)
```

```python
import functools
import math

import jax
import jax.numpy as jnp
from jax import lax
from jax.experimental import pallas as pl
from jax.experimental.pallas import tpu as pltpu
from jax.sharding import PartitionSpec as P

KERNEL = 7


EPSILON = 1e-06


MESH = pl.DeviceIdType.MESH
EDGE = 16


def barrier_with(peers):
    barrier = pltpu.get_barrier_semaphore()
    for peer in peers:
        pl.semaphore_signal(barrier, inc=1, device_id=peer, device_id_type=MESH)
    pl.semaphore_wait(barrier, len(peers))


def halo_kernel(lat_count, lon_count, radius, x_ref, wide_ref, send_sem, recv_sem):
    lat, lon = lax.axis_index("lat"), lax.axis_index("lon")
    rows, cols = x_ref.shape[0], x_ref.shape[1]
    row_from = {0: (0, radius, rows), 1: (rows - radius, 0, radius), -1: (0, rows + radius, radius)}
    col_from = {0: (0, EDGE, cols), 1: (cols - EDGE, 0, EDGE), -1: (0, cols + EDGE, EDGE)}
    ways = [(i, j) for i in (0, 1, -1) for j in (0, 1, -1) if (i, j) != (0, 0)]
    peers = [
        (lax.rem(lat + i + lat_count, lat_count), lax.rem(lon + j + lon_count, lon_count))
        for i, j in ways
    ]
    barrier_with(peers)
    copies = []
    for at, ((i, j), peer) in enumerate(zip(ways, peers)):
        row_src, row_dst, row_n = row_from[i]
        col_src, col_dst, col_n = col_from[j]
        copy = pltpu.make_async_remote_copy(
            src_ref=x_ref.at[pl.ds(row_src, row_n), pl.ds(col_src, col_n)],
            dst_ref=wide_ref.at[pl.ds(row_dst, row_n), pl.ds(col_dst, col_n)],
            send_sem=send_sem.at[at],
            recv_sem=recv_sem.at[at],
            device_id=peer,
            device_id_type=MESH,
        )
        copy.start()
        copies.append(copy)
    wide_ref[radius : radius + rows, EDGE : EDGE + cols] = x_ref[...]
    for copy in copies:
        copy.wait()

    @pl.when(lat == 0)
    def _():
        wide_ref[:radius] = jnp.zeros((radius,) + wide_ref.shape[1:], wide_ref.dtype)

    @pl.when(lat == lat_count - 1)
    def _():
        wide_ref[rows + radius :] = jnp.zeros((radius,) + wide_ref.shape[1:], wide_ref.dtype)


def rim_field(tile_field, collective_id):
    radius = KERNEL // 2
    rows, cols, channels = tile_field.shape
    wide = pl.pallas_call(
        functools.partial(halo_kernel, lax.axis_size("lat"), lax.axis_size("lon"), radius),
        out_shape=jax.ShapeDtypeStruct(
            (rows + 2 * radius, cols + 2 * EDGE, channels), tile_field.dtype
        ),
        in_specs=[pl.BlockSpec(memory_space=pltpu.VMEM)],
        out_specs=pl.BlockSpec(memory_space=pltpu.VMEM),
        scratch_shapes=[pltpu.SemaphoreType.DMA((8,)), pltpu.SemaphoreType.DMA((8,))],
        compiler_params=pltpu.CompilerParams(
            collective_id=collective_id, has_side_effects=True, vmem_limit_bytes=8 << 20
        ),
    )(tile_field)
    return wide[:, EDGE - radius : EDGE + cols + radius]


def reduce_kernel(bands, lon_count, scale, *refs):
    arrays = (len(refs) - 2) // 7
    group = [refs[i * arrays : (i + 1) * arrays] for i in range(7)]
    ins, outs, got1, sum1, got2, sum2, got3 = group
    send_sem, recv_sem = refs[-2:]
    lat, lon = lax.axis_index("lat"), lax.axis_index("lon")
    core, band = lax.rem(lat, 2), lax.div(lat, 2)
    pair = (lat + 1 - 2 * core, lon)
    others = [lax.rem(band + k, bands) for k in range(1, bands)]
    along = [lax.rem(lon + k, lon_count) for k in range(1, lon_count)]
    barrier_with([pair] + [(2 * b + core, lon) for b in others] + [(lat, m) for m in along])
    sems = iter(range(send_sem.shape[0]))

    def send(src, dst, peer):
        at = next(sems)
        copy = pltpu.make_async_remote_copy(
            src_ref=src,
            dst_ref=dst,
            send_sem=send_sem.at[at],
            recv_sem=recv_sem.at[at],
            device_id=peer,
            device_id_type=MESH,
        )
        copy.start()
        return copy

    first = [
        send(i.at[:, 1 - core], g, pair)
        for i, g in zip(ins, got1)
    ]
    for at, copy in enumerate(first):
        copy.wait()
        mine = ins[at][:, pl.ds(core, 1)][:, 0]
        sum1[at][...] = (
            mine.astype(jnp.float32) + got1[at][...].astype(jnp.float32)
        ).astype(jnp.bfloat16)
    second = [
        [
            send(s.at[b], g.at[k], (2 * b + core, lon))
            for k, b in enumerate(others)
        ]
        for s, g in zip(sum1, got2)
    ]
    third = []
    for at, copies in enumerate(second):
        total = sum1[at][pl.ds(band, 1)][0].astype(jnp.float32)
        for k, copy in enumerate(copies):
            copy.wait()
            total = total + got2[at][k].astype(jnp.float32)
        sum2[at][...] = total.astype(jnp.bfloat16)
        third.append([
            send(sum2[at].at[m], got3[at].at[k], (lat, m))
            for k, m in enumerate(along)
        ])
    for at, copies in enumerate(third):
        total = sum2[at][pl.ds(lon, 1)][0].astype(jnp.float32)
        for k, copy in enumerate(copies):
            copy.wait()
            total = total + got3[at][k].astype(jnp.float32)
        outs[at][...] = total * scale


def reduce_shares(arrays, scale, collective_id):
    lat_count, lon_count = lax.axis_size("lat"), lax.axis_size("lon")
    bands = lat_count // 2
    ins = [a.reshape((bands, 2, lon_count) + a.shape[1:]) for a in arrays]
    tails = [a.shape[1:] for a in arrays]
    copies = len(arrays) * (1 + (bands - 1) + (lon_count - 1))

    def scratch(*lead):
        return [pltpu.VMEM(lead + t, jnp.bfloat16) for t in tails]

    vmem = pl.BlockSpec(memory_space=pltpu.VMEM)
    return pl.pallas_call(
        functools.partial(reduce_kernel, bands, lon_count, scale),
        out_shape=[jax.ShapeDtypeStruct(t, jnp.float32) for t in tails],
        in_specs=[vmem] * len(ins),
        out_specs=[vmem] * len(ins),
        scratch_shapes=scratch(bands, lon_count)
        + scratch(bands, lon_count)
        + scratch(bands - 1, lon_count)
        + scratch(lon_count)
        + scratch(lon_count - 1)
        + [pltpu.SemaphoreType.DMA((copies,)), pltpu.SemaphoreType.DMA((copies,))],
        compiler_params=pltpu.CompilerParams(
            collective_id=collective_id, has_side_effects=True, vmem_limit_bytes=32 << 20
        ),
    )(*ins)


def packed_shares(grads, device_count, width):
    parts = [
        jnp.pad(
            g.astype(jnp.bfloat16).reshape(device_count, -1, g.shape[1]),
            ((0, 0), (0, 0), (0, width - g.shape[1])),
        )
        for g in grads
    ]
    rows = sum(p.shape[1] for p in parts)
    parts.append(jnp.zeros((device_count, -rows % 16, width), jnp.bfloat16))
    return jnp.concatenate(parts, axis=1)


def gelu_fn(values_in):
    return jax.nn.gelu(values_in, approximate=True)


def gelu_back(pre_act, upstream):
    return jax.vjp(gelu_fn, pre_act)[1](upstream)[0]


def depthwise(padded, kernel, row_count, col_count):
    summed = jnp.zeros((row_count, col_count, padded.shape[2]), jnp.float32)
    for row_off in range(kernel.shape[0]):
        for col_off in range(kernel.shape[1]):
            window = padded[row_off : row_off + row_count, col_off : col_off + col_count].astype(
                jnp.float32
            )
            summed = summed + kernel[row_off, col_off].astype(jnp.float32) * window
    return summed


def back_conv(wide_grad, kernel, row_count, col_count):
    kernel_span = kernel.shape[0] - 1
    summed = jnp.zeros((row_count, col_count, wide_grad.shape[2]), jnp.float32)
    for row_off in range(kernel.shape[0]):
        for col_off in range(kernel.shape[1]):
            low_row = kernel_span - row_off
            low_col = kernel_span - col_off
            window = wide_grad[low_row : low_row + row_count, low_col : low_col + col_count].astype(
                jnp.float32
            )
            summed = summed + kernel[row_off, col_off].astype(jnp.float32) * window
    return summed


def kernel_terms(wide_field, grad_field, kernel_size):
    row_count = grad_field.shape[0]
    col_count = grad_field.shape[1]
    terms_list = []
    for row_off in range(kernel_size):
        for col_off in range(kernel_size):
            window = wide_field[
                row_off : row_off + row_count, col_off : col_off + col_count
            ].astype(jnp.float32)
            terms_list.append(jnp.sum(grad_field * window, axis=(0, 1)))
    return jnp.stack(terms_list).reshape(kernel_size, kernel_size, grad_field.shape[2])


def physics_forward(col_rows, column_in, column_out):
    column_pre = jnp.dot(col_rows, column_in, preferred_element_type=jnp.float32)
    inner = gelu_fn(column_pre).astype(jnp.bfloat16)
    state_full = col_rows.astype(jnp.float32) + jnp.dot(
        inner, column_out, preferred_element_type=jnp.float32
    )
    return (column_pre, inner, state_full)


def physics_backward(col_rows, column_pre, inner, target, column_in, column_out):
    inner_back = jnp.dot(target, column_out.T, preferred_element_type=jnp.float32)
    column_pre_grad = gelu_back(column_pre, inner_back).astype(jnp.bfloat16)
    column_grad = (
        target.astype(jnp.float32)
        + jnp.dot(column_pre_grad, column_in.T, preferred_element_type=jnp.float32)
    ).astype(jnp.bfloat16)
    grad_cin = jnp.dot(column_pre_grad.T, col_rows, preferred_element_type=jnp.float32)
    grad_cout = jnp.dot(inner.T, target, preferred_element_type=jnp.float32)
    return (column_grad, grad_cin, grad_cout)


def local(
    latent,
    ocean_mask,
    depth_kernel,
    expand_weight,
    reduce_weight,
    decode_weight,
    column_in,
    column_out,
    state_cot,
):
    tile_rows, tile_cols, channels = latent.shape
    cell_count = tile_rows * tile_cols
    col_width = state_cot.shape[2]
    device_count = lax.axis_size("lat") * lax.axis_size("lon")
    grad_scale = 1.0 / math.sqrt(cell_count * device_count)
    ocean = ocean_mask.astype(latent.dtype)
    masked = latent * ocean[:, :, None]
    wide_field = rim_field(masked, 0)
    convolved = depthwise(wide_field, depth_kernel, tile_rows, tile_cols).reshape(
        cell_count, channels
    )
    row_mean = jnp.mean(convolved, axis=1, keepdims=True)
    centred = convolved - row_mean
    inverse_scale = lax.rsqrt(jnp.mean(centred * centred, axis=1, keepdims=True) + EPSILON)
    unit_rows = centred * inverse_scale
    normed = unit_rows.astype(jnp.bfloat16)
    expand_pre = jnp.dot(normed, expand_weight, preferred_element_type=jnp.float32)
    hidden = gelu_fn(expand_pre).astype(jnp.bfloat16)
    masked_flat = masked.reshape(cell_count, channels)
    feature = (
        masked_flat.astype(jnp.float32)
        + jnp.dot(hidden, reduce_weight, preferred_element_type=jnp.float32)
    ).astype(jnp.bfloat16)
    column = jnp.dot(feature, decode_weight, preferred_element_type=jnp.float32).astype(
        jnp.bfloat16
    )
    ocean_flat = ocean_mask.reshape(cell_count)
    cot_flat = state_cot.reshape(cell_count, col_width)
    ocean_rows = ocean_flat.astype(jnp.float32)[:, None]
    column_pre, inner, state_full = physics_forward(column, column_in, column_out)
    state_home = (ocean_rows * state_full).astype(jnp.bfloat16)
    target = (cot_flat.astype(jnp.float32) * ocean_rows).astype(jnp.bfloat16)
    column_grad, grad_cin, grad_cout = physics_backward(
        column, column_pre, inner, target, column_in, column_out
    )
    feature_back = jnp.dot(column_grad, decode_weight.T, preferred_element_type=jnp.float32)
    feature_grad = feature_back.astype(jnp.bfloat16)
    hidden_back = jnp.dot(feature_grad, reduce_weight.T, preferred_element_type=jnp.float32)
    expand_grad = gelu_back(expand_pre, hidden_back).astype(jnp.bfloat16)
    normed_back = jnp.dot(expand_grad, expand_weight.T, preferred_element_type=jnp.float32)
    conv_grad = (
        inverse_scale
        * (
            normed_back
            - jnp.mean(normed_back, axis=1, keepdims=True)
            - unit_rows * jnp.mean(normed_back * unit_rows, axis=1, keepdims=True)
        )
    ).astype(jnp.bfloat16)
    conv_tile = conv_grad.reshape(tile_rows, tile_cols, channels)
    wide_grad = rim_field(conv_tile, 1)
    grad_kernel = kernel_terms(wide_field, conv_tile.astype(jnp.float32), depth_kernel.shape[0])
    back_terms = back_conv(wide_grad, depth_kernel, tile_rows, tile_cols)
    grad_latent = (
        ocean_mask.astype(jnp.float32)[:, :, None]
        * (feature_back.reshape(tile_rows, tile_cols, channels) + back_terms)
    ).astype(jnp.bfloat16)
    grad_expand = jnp.dot(expand_grad.T, normed, preferred_element_type=jnp.float32)
    grad_reduce = jnp.dot(hidden.T, feature_grad, preferred_element_type=jnp.float32)
    grad_decode = jnp.dot(feature.T, column_grad, preferred_element_type=jnp.float32)
    kernel_rows = grad_kernel.reshape(-1, channels).T
    narrow, broad = reduce_shares(
        (
            packed_shares((grad_expand, grad_reduce), device_count, channels),
            packed_shares((grad_cin, grad_cout, grad_decode, kernel_rows), device_count, col_width),
        ),
        grad_scale,
        2,
    )
    hidden_share = grad_expand.shape[0] // device_count
    inner_share = grad_cin.shape[0] // device_count
    chan_share = channels // device_count
    tail = 2 * inner_share
    taps = depth_kernel.shape[:2]
    return (
        state_home.reshape(tile_rows, tile_cols, col_width),
        grad_latent,
        broad[tail + chan_share : tail + 2 * chan_share, : taps[0] * taps[1]]
        .T.reshape(taps + (chan_share,)),
        narrow[:hidden_share].T,
        narrow[hidden_share : 2 * hidden_share],
        broad[tail : tail + chan_share],
        broad[:inner_share].T,
        broad[inner_share:tail],
    )


def solution(mesh):
    in_specs = (
        P("lat", "lon", None),
        P("lat", "lon"),
        P(),
        P(),
        P(),
        P(),
        P(),
        P(),
        P("lat", "lon", None),
    )
    out_specs = (
        P("lat", "lon", None),
        P("lat", "lon", None),
        P(None, None, ("lat", "lon")),
        P(None, ("lat", "lon")),
        P(("lat", "lon"), None),
        P(("lat", "lon"), None),
        P(None, ("lat", "lon")),
        P(("lat", "lon"), None),
    )
    return jax.shard_map(local, mesh=mesh, in_specs=in_specs, out_specs=out_specs, check_vma=False)
```

```python
import functools
import math

import jax
import jax.numpy as jnp
from jax import lax
from jax.experimental import pallas as pl
from jax.experimental.pallas import tpu as pltpu
from jax.sharding import PartitionSpec as P

KERNEL = 7


EPSILON = 1e-06


MESH = pl.DeviceIdType.MESH
SIDE = 8


def barrier_with(peers):
    barrier = pltpu.get_barrier_semaphore()
    for peer in peers:
        pl.semaphore_signal(barrier, inc=1, device_id=peer, device_id_type=MESH)
    pl.semaphore_wait(barrier, len(peers))


def sender(send_sem, recv_sem):
    slots = iter(range(send_sem.shape[0]))

    def send(src, dst, peer):
        at = next(slots)
        copy = pltpu.make_async_remote_copy(
            src_ref=src,
            dst_ref=dst,
            send_sem=send_sem.at[at],
            recv_sem=recv_sem.at[at],
            device_id=peer,
            device_id_type=MESH,
        )
        copy.start()
        return copy

    return send


WAYS = [(i, j) for i in (0, 1, -1) for j in (0, 1, -1) if (i, j) != (0, 0)]


def rim_peers(lat_count, lon_count):
    lat, lon = lax.axis_index("lat"), lax.axis_index("lon")
    return [
        (lax.rem(lat + i + lat_count, lat_count), lax.rem(lon + j + lon_count, lon_count))
        for i, j in WAYS
    ]


def send_rim(send, peers, radius, x_ref, edge_ref, got_rows, got_edges):
    rows = x_ref.shape[0]
    copies = []
    for (i, j), peer in zip(WAYS, peers):
        if j == 0:
            first, slot = (rows - radius, 0) if i == 1 else (0, 1)
            copies.append(send(x_ref.at[pl.ds(first, radius)], got_rows.at[slot], peer))
        else:
            side = 1 if j == 1 else 0
            copies.append(send(edge_ref.at[side], got_edges.at[1 - side, i + 1], peer))
    return copies


def fill_tile(radius, x_ref, wide):
    rows, cols, channels = x_ref.shape
    for at in (0, SIDE + cols):
        wide[:, at : at + SIDE] = jnp.zeros((wide.shape[0], SIDE, channels), wide.dtype)

    @pl.loop(0, rows)
    def _(row):
        wide[row + radius, SIDE : SIDE + cols] = x_ref[row].astype(jnp.float32)


def fill_rim(lat_count, radius, x_ref, wide, got_rows, got_edges):
    rows, cols, channels = x_ref.shape
    lat = lax.axis_index("lat")
    for slot, low in ((0, 0), (1, rows + radius)):
        for r in range(radius):
            wide[low + r, SIDE : SIDE + cols] = got_rows[slot, r].astype(jnp.float32)
    for side, left in ((0, SIDE - radius), (1, SIDE + cols)):
        for i, first, low, count in (
            (0, 0, radius, rows),
            (1, rows - radius, 0, radius),
            (-1, 0, rows + radius, radius),
        ):
            for col in range(radius):
                block = got_edges[side, i + 1, col].astype(jnp.float32)
                for r in range(count):
                    wide[low + r, left + col : left + col + 1] = block[first + r : first + r + 1]
    for edge, low in ((0, 0), (lat_count - 1, rows + radius)):

        @pl.when(lat == edge)
        def _():
            wide[low : low + radius] = jnp.zeros((radius,) + wide.shape[1:], wide.dtype)


def conv_rows(wide, taps_ref, out_ref, low, high):
    cols, channels = out_ref.shape[1:]
    width = wide.shape[1]

    @pl.loop(low, high)
    def _(row):
        for lane in range(0, channels, 128):
            lanes = slice(lane, lane + 128)
            total = None
            for b in range(KERNEL):
                part = None
                for a in range(KERNEL):
                    field = wide[row + a, :, lanes].reshape(width // 8, 8, 128)
                    term = field * taps_ref[a * KERNEL + b, :, lanes][None]
                    part = term if part is None else part + term
                first = SIDE - KERNEL // 2 + b
                part = part.reshape(width, 128)[first : first + cols]
                total = part if total is None else total + part
            out_ref[row, :, lanes] = total


def forward_kernel(
    lat_count, lon_count, x_ref, edge_ref, taps_ref, out_ref, field_ref,
    wide, got_rows, got_edges, send_sem, recv_sem,
):
    radius = KERNEL // 2
    peers = rim_peers(lat_count, lon_count)
    barrier_with(peers)
    copies = send_rim(
        sender(send_sem, recv_sem), peers, radius, x_ref, edge_ref, got_rows, got_edges
    )
    fill_tile(radius, x_ref, wide)
    for copy in copies:
        copy.wait()
    fill_rim(lat_count, radius, x_ref, wide, got_rows, got_edges)

    @pl.loop(0, wide.shape[0])
    def _(row):
        field_ref[row] = wide[row].astype(jnp.bfloat16)

    conv_rows(wide, taps_ref, out_ref, 0, x_ref.shape[0])


def backward_kernel(
    lat_count, lon_count, scale, x_ref, edge_ref, taps_ref, narrow_ref, broad_ref,
    out_ref, narrow_out, broad_out,
    wide, got_rows, got_edges, n_got1, n_sum1, n_got2, n_sum2, n_got3,
    b_got1, b_sum1, b_got2, b_sum2, b_got3, send_sem, recv_sem,
):
    radius = KERNEL // 2
    rows = x_ref.shape[0]
    bands = lat_count // 2
    lat, lon = lax.axis_index("lat"), lax.axis_index("lon")
    core, band = lax.rem(lat, 2), lax.div(lat, 2)
    pair = (lat + 1 - 2 * core, lon)
    others = [lax.rem(band + k, bands) for k in range(1, bands)]
    along = [lax.rem(lon + k, lon_count) for k in range(1, lon_count)]
    peers = rim_peers(lat_count, lon_count)
    other_peers = [(2 * b + core, lon) for b in others]
    along_peers = [(lat, m) for m in along]
    barrier_with(peers + [pair] + other_peers + along_peers)
    send = sender(send_sem, recv_sem)

    def wide_sum(*terms):
        total = terms[0].astype(jnp.float32)
        for term in terms[1:]:
            total = total + term.astype(jnp.float32)
        return total

    first = [
        send(ref.at[:, 1 - core], got, pair)
        for ref, got in ((narrow_ref, n_got1), (broad_ref, b_got1))
    ]
    rim = send_rim(send, peers, radius, x_ref, edge_ref, got_rows, got_edges)
    fill_tile(radius, x_ref, wide)
    for copy, ref, got, total in zip(
        first, (narrow_ref, broad_ref), (n_got1, b_got1), (n_sum1, b_sum1)
    ):
        copy.wait()
        for b in range(bands):
            total[b] = wide_sum(ref[b, core], got[b]).astype(jnp.bfloat16)
    n_second = [
        send(n_sum1.at[:, m], n_got2.at[k], peer)
        for k, (m, peer) in enumerate(zip(along, along_peers))
    ]
    b_second = [
        send(b_sum1.at[b], b_got2.at[k], peer)
        for k, (b, peer) in enumerate(zip(others, other_peers))
    ]
    for copy in rim:
        copy.wait()
    fill_rim(lat_count, radius, x_ref, wide, got_rows, got_edges)
    conv_rows(wide, taps_ref, out_ref, 0, rows // 2)
    for copy in b_second:
        copy.wait()
    b_sum2[...] = wide_sum(b_sum1[band], *[b_got2[k] for k in range(bands - 1)]).astype(
        jnp.bfloat16
    )
    b_third = [
        send(b_sum2.at[m], b_got3.at[k], peer)
        for k, (m, peer) in enumerate(zip(along, along_peers))
    ]
    for copy in n_second:
        copy.wait()
    for b in range(bands):
        n_sum2[b] = wide_sum(
            n_sum1[b, lon], *[n_got2[k, b] for k in range(lon_count - 1)]
        ).astype(jnp.bfloat16)
    n_third = [
        send(n_sum2.at[b], n_got3.at[k], peer)
        for k, (b, peer) in enumerate(zip(others, other_peers))
    ]
    conv_rows(wide, taps_ref, out_ref, rows // 2, rows)
    for copy in n_third:
        copy.wait()
    narrow_out[...] = scale * wide_sum(n_sum2[band], *[n_got3[k] for k in range(bands - 1)])
    for copy in b_third:
        copy.wait()
    broad_out[...] = scale * wide_sum(b_sum2[lon], *[b_got3[k] for k in range(lon_count - 1)])


def edge_columns(cells):
    radius = KERNEL // 2
    sides = (cells[:, :radius], cells[:, cells.shape[1] - radius :])
    return jnp.stack([jnp.transpose(s, (1, 0, 2)) for s in sides])


def tap_rows(kernel):
    taps = kernel.astype(jnp.float32).reshape(KERNEL * KERNEL, 1, kernel.shape[2])
    return jnp.broadcast_to(taps, (KERNEL * KERNEL, 8, kernel.shape[2]))


def rim_scratch(tile):
    rows, cols, channels = tile.shape
    radius = KERNEL // 2
    return [
        pltpu.VMEM((rows + 2 * radius, cols + 2 * SIDE, channels), jnp.float32),
        pltpu.VMEM((2, radius, cols, channels), jnp.bfloat16),
        pltpu.VMEM((2, 3, radius, rows, channels), jnp.bfloat16),
    ]


VMEM_SPEC = pl.BlockSpec(memory_space=pltpu.VMEM)


def forward_conv(tile, kernel):
    rows, cols, channels = tile.shape
    radius = KERNEL // 2
    convolved, field = pl.pallas_call(
        functools.partial(forward_kernel, lax.axis_size("lat"), lax.axis_size("lon")),
        out_shape=[
            jax.ShapeDtypeStruct(tile.shape, jnp.float32),
            jax.ShapeDtypeStruct((rows + 2 * radius, cols + 2 * SIDE, channels), jnp.bfloat16),
        ],
        in_specs=[VMEM_SPEC] * 3,
        out_specs=[VMEM_SPEC] * 2,
        scratch_shapes=rim_scratch(tile)
        + [pltpu.SemaphoreType.DMA((8,)), pltpu.SemaphoreType.DMA((8,))],
        compiler_params=pltpu.CompilerParams(
            collective_id=0, has_side_effects=True, vmem_limit_bytes=24 << 20
        ),
    )(tile, edge_columns(tile), tap_rows(kernel))
    return convolved, field[:, SIDE - radius : SIDE + cols + radius]


def backward_conv(tile, kernel, narrow, broad, scale):
    lat_count, lon_count = lax.axis_size("lat"), lax.axis_size("lon")
    bands = lat_count // 2
    shares = [a.reshape((bands, 2, lon_count) + a.shape[1:]) for a in (narrow, broad)]
    n_tail, b_tail = narrow.shape[1:], broad.shape[1:]
    copies = 8 + 2 * (1 + (bands - 1) + (lon_count - 1))

    def scratch(tail, *leads):
        return [pltpu.VMEM(lead + tail, jnp.bfloat16) for lead in leads]

    return pl.pallas_call(
        functools.partial(backward_kernel, lat_count, lon_count, scale),
        out_shape=[
            jax.ShapeDtypeStruct(tile.shape, jnp.float32),
            jax.ShapeDtypeStruct(n_tail, jnp.float32),
            jax.ShapeDtypeStruct(b_tail, jnp.float32),
        ],
        in_specs=[VMEM_SPEC] * 5,
        out_specs=[VMEM_SPEC] * 3,
        scratch_shapes=rim_scratch(tile)
        + scratch(
            n_tail, (bands, lon_count), (bands, lon_count), (lon_count - 1, bands), (bands,),
            (bands - 1,),
        )
        + scratch(
            b_tail, (bands, lon_count), (bands, lon_count), (bands - 1, lon_count), (lon_count,),
            (lon_count - 1,),
        )
        + [pltpu.SemaphoreType.DMA((copies,)), pltpu.SemaphoreType.DMA((copies,))],
        compiler_params=pltpu.CompilerParams(
            collective_id=1, has_side_effects=True, vmem_limit_bytes=40 << 20
        ),
    )(tile, edge_columns(tile), tap_rows(kernel[::-1, ::-1]), *shares)


def packed_shares(grads, device_count, width):
    parts = [
        jnp.pad(
            g.astype(jnp.bfloat16).reshape(device_count, -1, g.shape[1]),
            ((0, 0), (0, 0), (0, width - g.shape[1])),
        )
        for g in grads
    ]
    rows = sum(p.shape[1] for p in parts)
    parts.append(jnp.zeros((device_count, -rows % 16, width), jnp.bfloat16))
    return jnp.concatenate(parts, axis=1)


def gelu_fn(values_in):
    return jax.nn.gelu(values_in, approximate=True)


def gelu_back(pre_act, upstream):
    return jax.vjp(gelu_fn, pre_act)[1](upstream)[0]


def kernel_terms(wide_field, grad_field, kernel_size):
    row_count = grad_field.shape[0]
    col_count = grad_field.shape[1]
    terms_list = []
    for row_off in range(kernel_size):
        for col_off in range(kernel_size):
            window = wide_field[
                row_off : row_off + row_count, col_off : col_off + col_count
            ].astype(jnp.float32)
            terms_list.append(jnp.sum(grad_field * window, axis=(0, 1)))
    return jnp.stack(terms_list).reshape(kernel_size, kernel_size, grad_field.shape[2])


def physics_forward(col_rows, column_in, column_out):
    column_pre = jnp.dot(col_rows, column_in, preferred_element_type=jnp.float32)
    inner = gelu_fn(column_pre).astype(jnp.bfloat16)
    state_full = col_rows.astype(jnp.float32) + jnp.dot(
        inner, column_out, preferred_element_type=jnp.float32
    )
    return (column_pre, inner, state_full)


def physics_backward(col_rows, column_pre, inner, target, column_in, column_out):
    inner_back = jnp.dot(target, column_out.T, preferred_element_type=jnp.float32)
    column_pre_grad = gelu_back(column_pre, inner_back).astype(jnp.bfloat16)
    column_grad = (
        target.astype(jnp.float32)
        + jnp.dot(column_pre_grad, column_in.T, preferred_element_type=jnp.float32)
    ).astype(jnp.bfloat16)
    grad_cin = jnp.dot(column_pre_grad.T, col_rows, preferred_element_type=jnp.float32)
    grad_cout = jnp.dot(inner.T, target, preferred_element_type=jnp.float32)
    return (column_grad, grad_cin, grad_cout)


def local(
    latent,
    ocean_mask,
    depth_kernel,
    expand_weight,
    reduce_weight,
    decode_weight,
    column_in,
    column_out,
    state_cot,
):
    tile_rows, tile_cols, channels = latent.shape
    cell_count = tile_rows * tile_cols
    col_width = state_cot.shape[2]
    device_count = lax.axis_size("lat") * lax.axis_size("lon")
    grad_scale = 1.0 / math.sqrt(cell_count * device_count)
    ocean = ocean_mask.astype(latent.dtype)
    masked = latent * ocean[:, :, None]
    convolved, wide_field = forward_conv(masked, depth_kernel)
    convolved = convolved.reshape(cell_count, channels)
    row_mean = jnp.mean(convolved, axis=1, keepdims=True)
    centred = convolved - row_mean
    inverse_scale = lax.rsqrt(jnp.mean(centred * centred, axis=1, keepdims=True) + EPSILON)
    unit_rows = centred * inverse_scale
    normed = unit_rows.astype(jnp.bfloat16)
    expand_pre = jnp.dot(normed, expand_weight, preferred_element_type=jnp.float32)
    hidden = gelu_fn(expand_pre).astype(jnp.bfloat16)
    masked_flat = masked.reshape(cell_count, channels)
    feature = (
        masked_flat.astype(jnp.float32)
        + jnp.dot(hidden, reduce_weight, preferred_element_type=jnp.float32)
    ).astype(jnp.bfloat16)
    column = jnp.dot(feature, decode_weight, preferred_element_type=jnp.float32).astype(
        jnp.bfloat16
    )
    ocean_flat = ocean_mask.reshape(cell_count)
    cot_flat = state_cot.reshape(cell_count, col_width)
    ocean_rows = ocean_flat.astype(jnp.float32)[:, None]
    column_pre, inner, state_full = physics_forward(column, column_in, column_out)
    state_home = (ocean_rows * state_full).astype(jnp.bfloat16)
    target = (cot_flat.astype(jnp.float32) * ocean_rows).astype(jnp.bfloat16)
    column_grad, grad_cin, grad_cout = physics_backward(
        column, column_pre, inner, target, column_in, column_out
    )
    feature_back = jnp.dot(column_grad, decode_weight.T, preferred_element_type=jnp.float32)
    feature_grad = feature_back.astype(jnp.bfloat16)
    hidden_back = jnp.dot(feature_grad, reduce_weight.T, preferred_element_type=jnp.float32)
    expand_grad = gelu_back(expand_pre, hidden_back).astype(jnp.bfloat16)
    normed_back = jnp.dot(expand_grad, expand_weight.T, preferred_element_type=jnp.float32)
    conv_grad = (
        inverse_scale
        * (
            normed_back
            - jnp.mean(normed_back, axis=1, keepdims=True)
            - unit_rows * jnp.mean(normed_back * unit_rows, axis=1, keepdims=True)
        )
    ).astype(jnp.bfloat16)
    conv_tile = conv_grad.reshape(tile_rows, tile_cols, channels)
    grad_kernel = kernel_terms(wide_field, conv_tile.astype(jnp.float32), depth_kernel.shape[0])
    grad_expand = jnp.dot(expand_grad.T, normed, preferred_element_type=jnp.float32)
    grad_reduce = jnp.dot(hidden.T, feature_grad, preferred_element_type=jnp.float32)
    grad_decode = jnp.dot(feature.T, column_grad, preferred_element_type=jnp.float32)
    kernel_rows = grad_kernel.reshape(-1, channels).T
    back_terms, narrow, broad = backward_conv(
        conv_tile,
        depth_kernel,
        packed_shares((grad_expand, grad_reduce), device_count, channels),
        packed_shares((grad_cin, grad_cout, grad_decode, kernel_rows), device_count, col_width),
        grad_scale,
    )
    grad_latent = (
        ocean_mask.astype(jnp.float32)[:, :, None]
        * (feature_back.reshape(tile_rows, tile_cols, channels) + back_terms)
    ).astype(jnp.bfloat16)
    hidden_share = grad_expand.shape[0] // device_count
    inner_share = grad_cin.shape[0] // device_count
    chan_share = channels // device_count
    tail = 2 * inner_share
    taps = depth_kernel.shape[:2]
    return (
        state_home.reshape(tile_rows, tile_cols, col_width),
        grad_latent,
        broad[tail + chan_share : tail + 2 * chan_share, : taps[0] * taps[1]]
        .T.reshape(taps + (chan_share,)),
        narrow[:hidden_share].T,
        narrow[hidden_share : 2 * hidden_share],
        broad[tail : tail + chan_share],
        broad[:inner_share].T,
        broad[inner_share:tail],
    )


def solution(mesh):
    in_specs = (
        P("lat", "lon", None),
        P("lat", "lon"),
        P(),
        P(),
        P(),
        P(),
        P(),
        P(),
        P("lat", "lon", None),
    )
    out_specs = (
        P("lat", "lon", None),
        P("lat", "lon", None),
        P(None, None, ("lat", "lon")),
        P(None, ("lat", "lon")),
        P(("lat", "lon"), None),
        P(("lat", "lon"), None),
        P(None, ("lat", "lon")),
        P(("lat", "lon"), None),
    )
    return jax.shard_map(local, mesh=mesh, in_specs=in_specs, out_specs=out_specs, check_vma=False)
```

```python
import functools
import math

import jax
import jax.numpy as jnp
from jax import lax
from jax.experimental import pallas as pl
from jax.experimental.pallas import tpu as pltpu
from jax.sharding import PartitionSpec as P

KERNEL = 7


EPSILON = 1e-06


MESH = pl.DeviceIdType.MESH
SIDE = 8


def barrier_with(peers):
    barrier = pltpu.get_barrier_semaphore()
    for peer in peers:
        pl.semaphore_signal(barrier, inc=1, device_id=peer, device_id_type=MESH)
    pl.semaphore_wait(barrier, len(peers))


def sender(send_sem, recv_sem):
    slots = iter(range(send_sem.shape[0]))

    def send(src, dst, peer):
        at = next(slots)
        copy = pltpu.make_async_remote_copy(
            src_ref=src,
            dst_ref=dst,
            send_sem=send_sem.at[at],
            recv_sem=recv_sem.at[at],
            device_id=peer,
            device_id_type=MESH,
        )
        copy.start()
        return copy

    return send


WAYS = [(i, j) for i in (0, 1, -1) for j in (0, 1, -1) if (i, j) != (0, 0)]


def rim_peers(lat_count, lon_count):
    lat, lon = lax.axis_index("lat"), lax.axis_index("lon")
    return [
        (lax.rem(lat + i + lat_count, lat_count), lax.rem(lon + j + lon_count, lon_count))
        for i, j in WAYS
    ]


def send_rim(send, peers, radius, x_ref, edge_ref, got_rows, got_edges):
    rows = x_ref.shape[0]
    copies = []
    for (i, j), peer in zip(WAYS, peers):
        if j == 0:
            first, slot = (rows - radius, 0) if i == 1 else (0, 1)
            copies.append(send(x_ref.at[pl.ds(first, radius)], got_rows.at[slot], peer))
        else:
            side = 1 if j == 1 else 0
            copies.append(send(edge_ref.at[side], got_edges.at[1 - side, i + 1], peer))
    return copies


def fill_tile(radius, x_ref, wide):
    rows, cols, channels = x_ref.shape
    for at in (0, SIDE + cols):
        wide[:, at : at + SIDE] = jnp.zeros((wide.shape[0], SIDE, channels), wide.dtype)

    @pl.loop(0, rows)
    def _(row):
        wide[row + radius, SIDE : SIDE + cols] = x_ref[row].astype(jnp.float32)


def fill_rim(lat_count, radius, x_ref, wide, got_rows, got_edges):
    rows, cols, channels = x_ref.shape
    lat = lax.axis_index("lat")
    for slot, low in ((0, 0), (1, rows + radius)):
        for r in range(radius):
            wide[low + r, SIDE : SIDE + cols] = got_rows[slot, r].astype(jnp.float32)
    for side, left in ((0, SIDE - radius), (1, SIDE + cols)):
        for i, first, low, count in (
            (0, 0, radius, rows),
            (1, rows - radius, 0, radius),
            (-1, 0, rows + radius, radius),
        ):
            for col in range(radius):
                block = got_edges[side, i + 1, col].astype(jnp.float32)
                for r in range(count):
                    wide[low + r, left + col : left + col + 1] = block[first + r : first + r + 1]
    for edge, low in ((0, 0), (lat_count - 1, rows + radius)):

        @pl.when(lat == edge)
        def _():
            wide[low : low + radius] = jnp.zeros((radius,) + wide.shape[1:], wide.dtype)


def conv_rows(wide, taps_ref, out_ref, low, high):
    cols, channels = out_ref.shape[1:]
    width = wide.shape[1]

    @pl.loop(low, high)
    def _(row):
        for lane in range(0, channels, 128):
            lanes = slice(lane, lane + 128)
            total = None
            for b in range(KERNEL):
                part = None
                for a in range(KERNEL):
                    field = wide[row + a, :, lanes].reshape(width // 8, 8, 128)
                    term = field * taps_ref[a * KERNEL + b, :, lanes][None]
                    part = term if part is None else part + term
                first = SIDE - KERNEL // 2 + b
                part = part.reshape(width, 128)[first : first + cols]
                total = part if total is None else total + part
            out_ref[row, :, lanes] = total


def forward_kernel(
    lat_count, lon_count, x_ref, edge_ref, taps_ref, out_ref, field_ref,
    wide, got_rows, got_edges, send_sem, recv_sem,
):
    radius = KERNEL // 2
    peers = rim_peers(lat_count, lon_count)
    barrier_with(peers)
    copies = send_rim(
        sender(send_sem, recv_sem), peers, radius, x_ref, edge_ref, got_rows, got_edges
    )
    fill_tile(radius, x_ref, wide)
    for copy in copies:
        copy.wait()
    fill_rim(lat_count, radius, x_ref, wide, got_rows, got_edges)

    @pl.loop(0, wide.shape[0])
    def _(row):
        field_ref[row] = wide[row].astype(jnp.bfloat16)

    conv_rows(wide, taps_ref, out_ref, 0, x_ref.shape[0])


def backward_kernel(
    lat_count, lon_count, scale, x_ref, edge_ref, taps_ref, narrow_ref, broad_ref,
    out_ref, narrow_out, broad_out,
    wide, got_rows, got_edges, n_got1, n_sum1, n_got2, n_sum2, n_got3,
    b_got1, b_sum1, b_got2, b_sum2, b_got3, send_sem, recv_sem,
):
    radius = KERNEL // 2
    rows = x_ref.shape[0]
    bands = lat_count // 2
    lat, lon = lax.axis_index("lat"), lax.axis_index("lon")
    core, band = lax.rem(lat, 2), lax.div(lat, 2)
    pair = (lat + 1 - 2 * core, lon)
    others = [lax.rem(band + k, bands) for k in range(1, bands)]
    along = [lax.rem(lon + k, lon_count) for k in range(1, lon_count)]
    peers = rim_peers(lat_count, lon_count)
    other_peers = [(2 * b + core, lon) for b in others]
    along_peers = [(lat, m) for m in along]
    barrier_with(peers + [pair] + other_peers + along_peers)
    send = sender(send_sem, recv_sem)

    def wide_sum(*terms):
        total = terms[0].astype(jnp.float32)
        for term in terms[1:]:
            total = total + term.astype(jnp.float32)
        return total

    first = [
        send(ref.at[:, 1 - core], got, pair)
        for ref, got in ((narrow_ref, n_got1), (broad_ref, b_got1))
    ]
    rim = send_rim(send, peers, radius, x_ref, edge_ref, got_rows, got_edges)
    fill_tile(radius, x_ref, wide)
    for copy, ref, got, total in zip(
        first, (narrow_ref, broad_ref), (n_got1, b_got1), (n_sum1, b_sum1)
    ):
        copy.wait()
        for b in range(bands):
            total[b] = wide_sum(ref[b, core], got[b]).astype(jnp.bfloat16)
    n_second = [
        send(n_sum1.at[:, m], n_got2.at[k], peer)
        for k, (m, peer) in enumerate(zip(along, along_peers))
    ]
    b_second = [
        send(b_sum1.at[b], b_got2.at[k], peer)
        for k, (b, peer) in enumerate(zip(others, other_peers))
    ]
    for copy in rim:
        copy.wait()
    fill_rim(lat_count, radius, x_ref, wide, got_rows, got_edges)
    conv_rows(wide, taps_ref, out_ref, 0, rows // 2)
    for copy in b_second:
        copy.wait()
    b_sum2[...] = wide_sum(b_sum1[band], *[b_got2[k] for k in range(bands - 1)]).astype(
        jnp.bfloat16
    )
    b_third = [
        send(b_sum2.at[m], b_got3.at[k], peer)
        for k, (m, peer) in enumerate(zip(along, along_peers))
    ]
    for copy in n_second:
        copy.wait()
    for b in range(bands):
        n_sum2[b] = wide_sum(
            n_sum1[b, lon], *[n_got2[k, b] for k in range(lon_count - 1)]
        ).astype(jnp.bfloat16)
    n_third = [
        send(n_sum2.at[b], n_got3.at[k], peer)
        for k, (b, peer) in enumerate(zip(others, other_peers))
    ]
    conv_rows(wide, taps_ref, out_ref, rows // 2, rows)
    for copy in n_third:
        copy.wait()
    narrow_out[...] = scale * wide_sum(n_sum2[band], *[n_got3[k] for k in range(bands - 1)])
    for copy in b_third:
        copy.wait()
    broad_out[...] = scale * wide_sum(b_sum2[lon], *[b_got3[k] for k in range(lon_count - 1)])


def edge_columns(cells):
    radius = KERNEL // 2
    sides = (cells[:, :radius], cells[:, cells.shape[1] - radius :])
    return jnp.stack([jnp.transpose(s, (1, 0, 2)) for s in sides])


def tap_rows(kernel):
    taps = kernel.astype(jnp.float32).reshape(KERNEL * KERNEL, 1, kernel.shape[2])
    return jnp.broadcast_to(taps, (KERNEL * KERNEL, 8, kernel.shape[2]))


def rim_scratch(tile):
    rows, cols, channels = tile.shape
    radius = KERNEL // 2
    return [
        pltpu.VMEM((rows + 2 * radius, cols + 2 * SIDE, channels), jnp.float32),
        pltpu.VMEM((2, radius, cols, channels), jnp.bfloat16),
        pltpu.VMEM((2, 3, radius, rows, channels), jnp.bfloat16),
    ]


VMEM_SPEC = pl.BlockSpec(memory_space=pltpu.VMEM)


def forward_conv(tile, kernel):
    rows, cols, channels = tile.shape
    radius = KERNEL // 2
    convolved, field = pl.pallas_call(
        functools.partial(forward_kernel, lax.axis_size("lat"), lax.axis_size("lon")),
        out_shape=[
            jax.ShapeDtypeStruct(tile.shape, jnp.float32),
            jax.ShapeDtypeStruct((rows + 2 * radius, cols + 2 * SIDE, channels), jnp.bfloat16),
        ],
        in_specs=[VMEM_SPEC] * 3,
        out_specs=[VMEM_SPEC] * 2,
        scratch_shapes=rim_scratch(tile)
        + [pltpu.SemaphoreType.DMA((8,)), pltpu.SemaphoreType.DMA((8,))],
        compiler_params=pltpu.CompilerParams(
            collective_id=0, has_side_effects=True, vmem_limit_bytes=24 << 20
        ),
    )(tile, edge_columns(tile), tap_rows(kernel))
    return convolved, field[:, SIDE - radius : SIDE + cols + radius]


def backward_conv(tile, kernel, narrow, broad, scale):
    lat_count, lon_count = lax.axis_size("lat"), lax.axis_size("lon")
    bands = lat_count // 2
    shares = [a.reshape((bands, 2, lon_count) + a.shape[1:]) for a in (narrow, broad)]
    n_tail, b_tail = narrow.shape[1:], broad.shape[1:]
    copies = 8 + 2 * (1 + (bands - 1) + (lon_count - 1))

    def scratch(tail, *leads):
        return [pltpu.VMEM(lead + tail, jnp.bfloat16) for lead in leads]

    return pl.pallas_call(
        functools.partial(backward_kernel, lat_count, lon_count, scale),
        out_shape=[
            jax.ShapeDtypeStruct(tile.shape, jnp.float32),
            jax.ShapeDtypeStruct(n_tail, jnp.float32),
            jax.ShapeDtypeStruct(b_tail, jnp.float32),
        ],
        in_specs=[VMEM_SPEC] * 5,
        out_specs=[VMEM_SPEC] * 3,
        scratch_shapes=rim_scratch(tile)
        + scratch(
            n_tail, (bands, lon_count), (bands, lon_count), (lon_count - 1, bands), (bands,),
            (bands - 1,),
        )
        + scratch(
            b_tail, (bands, lon_count), (bands, lon_count), (bands - 1, lon_count), (lon_count,),
            (lon_count - 1,),
        )
        + [pltpu.SemaphoreType.DMA((copies,)), pltpu.SemaphoreType.DMA((copies,))],
        compiler_params=pltpu.CompilerParams(
            collective_id=1, has_side_effects=True, vmem_limit_bytes=40 << 20
        ),
    )(tile, edge_columns(tile), tap_rows(kernel[::-1, ::-1]), *shares)


def packed_shares(grads, device_count, width):
    parts = [
        jnp.pad(
            g.astype(jnp.bfloat16).reshape(device_count, -1, g.shape[1]),
            ((0, 0), (0, 0), (0, width - g.shape[1])),
        )
        for g in grads
    ]
    rows = sum(p.shape[1] for p in parts)
    parts.append(jnp.zeros((device_count, -rows % 16, width), jnp.bfloat16))
    return jnp.concatenate(parts, axis=1)


def gelu_fn(values_in):
    return jax.nn.gelu(values_in, approximate=True)


def gelu_back(pre_act, upstream):
    rate = math.sqrt(2.0 / math.pi)
    square = pre_act * pre_act
    bend = (rate * 0.044715) * square
    t = jnp.tanh(pre_act * (rate + bend))
    slope = (0.5 * rate) + 1.5 * bend
    return upstream * ((0.5 + 0.5 * t) + (pre_act * slope) * (1.0 - t * t))


def kernel_terms(wide_field, grad_field, kernel_size):
    row_count = grad_field.shape[0]
    col_count = grad_field.shape[1]
    terms_list = []
    for row_off in range(kernel_size):
        for col_off in range(kernel_size):
            window = wide_field[
                row_off : row_off + row_count, col_off : col_off + col_count
            ].astype(jnp.float32)
            terms_list.append(jnp.sum(grad_field * window, axis=(0, 1)))
    return jnp.stack(terms_list).reshape(kernel_size, kernel_size, grad_field.shape[2])


def physics_forward(col_rows, column_in, column_out):
    column_pre = jnp.dot(col_rows, column_in, preferred_element_type=jnp.float32)
    inner = gelu_fn(column_pre).astype(jnp.bfloat16)
    state_full = col_rows.astype(jnp.float32) + jnp.dot(
        inner, column_out, preferred_element_type=jnp.float32
    )
    return (column_pre, inner, state_full)


def physics_backward(col_rows, column_pre, inner, target, column_in, column_out):
    inner_back = jnp.dot(target, column_out.T, preferred_element_type=jnp.float32)
    column_pre_grad = lax.optimization_barrier(
        gelu_back(column_pre, inner_back).astype(jnp.bfloat16)
    )
    column_grad = (
        target.astype(jnp.float32)
        + jnp.dot(column_pre_grad, column_in.T, preferred_element_type=jnp.float32)
    ).astype(jnp.bfloat16)
    grad_cin = jnp.dot(column_pre_grad.T, col_rows, preferred_element_type=jnp.float32)
    grad_cout = jnp.dot(inner.T, target, preferred_element_type=jnp.float32)
    return (column_grad, grad_cin, grad_cout)


def local(
    latent,
    ocean_mask,
    depth_kernel,
    expand_weight,
    reduce_weight,
    decode_weight,
    column_in,
    column_out,
    state_cot,
):
    tile_rows, tile_cols, channels = latent.shape
    cell_count = tile_rows * tile_cols
    col_width = state_cot.shape[2]
    device_count = lax.axis_size("lat") * lax.axis_size("lon")
    grad_scale = 1.0 / math.sqrt(cell_count * device_count)
    ocean = ocean_mask.astype(latent.dtype)
    masked = latent * ocean[:, :, None]
    convolved, wide_field = forward_conv(masked, depth_kernel)
    convolved = convolved.reshape(cell_count, channels)
    row_mean = jnp.mean(convolved, axis=1, keepdims=True)
    centred = convolved - row_mean
    inverse_scale = lax.rsqrt(jnp.mean(centred * centred, axis=1, keepdims=True) + EPSILON)
    unit_rows = centred * inverse_scale
    normed = unit_rows.astype(jnp.bfloat16)
    expand_pre = jnp.dot(normed, expand_weight, preferred_element_type=jnp.float32)
    hidden = gelu_fn(expand_pre).astype(jnp.bfloat16)
    masked_flat = masked.reshape(cell_count, channels)
    feature = (
        masked_flat.astype(jnp.float32)
        + jnp.dot(hidden, reduce_weight, preferred_element_type=jnp.float32)
    ).astype(jnp.bfloat16)
    column = jnp.dot(feature, decode_weight, preferred_element_type=jnp.float32).astype(
        jnp.bfloat16
    )
    ocean_flat = ocean_mask.reshape(cell_count)
    cot_flat = state_cot.reshape(cell_count, col_width)
    ocean_rows = ocean_flat.astype(jnp.float32)[:, None]
    column_pre, inner, state_full = physics_forward(column, column_in, column_out)
    state_home = (ocean_rows * state_full).astype(jnp.bfloat16)
    target = cot_flat * ocean_flat.astype(jnp.bfloat16)[:, None]
    column_grad, grad_cin, grad_cout = physics_backward(
        column, column_pre, inner, target, column_in, column_out
    )
    feature_back = jnp.dot(column_grad, decode_weight.T, preferred_element_type=jnp.float32)
    feature_grad = feature_back.astype(jnp.bfloat16)
    hidden_back = jnp.dot(feature_grad, reduce_weight.T, preferred_element_type=jnp.float32)
    expand_grad = lax.optimization_barrier(
        gelu_back(expand_pre, hidden_back).astype(jnp.bfloat16)
    )
    normed_back = jnp.dot(expand_grad, expand_weight.T, preferred_element_type=jnp.float32)
    conv_grad = (
        inverse_scale
        * (
            normed_back
            - jnp.mean(normed_back, axis=1, keepdims=True)
            - unit_rows * jnp.mean(normed_back * unit_rows, axis=1, keepdims=True)
        )
    ).astype(jnp.bfloat16)
    conv_tile = conv_grad.reshape(tile_rows, tile_cols, channels)
    grad_kernel = kernel_terms(wide_field, conv_tile.astype(jnp.float32), depth_kernel.shape[0])
    grad_expand = jnp.dot(expand_grad.T, normed, preferred_element_type=jnp.float32)
    grad_reduce = jnp.dot(hidden.T, feature_grad, preferred_element_type=jnp.float32)
    grad_decode = jnp.dot(feature.T, column_grad, preferred_element_type=jnp.float32)
    kernel_rows = grad_kernel.reshape(-1, channels).T
    back_terms, narrow, broad = backward_conv(
        conv_tile,
        depth_kernel,
        packed_shares((grad_expand, grad_reduce), device_count, channels),
        packed_shares((grad_cin, grad_cout, grad_decode, kernel_rows), device_count, col_width),
        grad_scale,
    )
    grad_latent = (
        ocean_mask.astype(jnp.float32)[:, :, None]
        * (feature_back.reshape(tile_rows, tile_cols, channels) + back_terms)
    ).astype(jnp.bfloat16)
    hidden_share = grad_expand.shape[0] // device_count
    inner_share = grad_cin.shape[0] // device_count
    chan_share = channels // device_count
    tail = 2 * inner_share
    taps = depth_kernel.shape[:2]
    return (
        state_home.reshape(tile_rows, tile_cols, col_width),
        grad_latent,
        broad[tail + chan_share : tail + 2 * chan_share, : taps[0] * taps[1]]
        .T.reshape(taps + (chan_share,)),
        narrow[:hidden_share].T,
        narrow[hidden_share : 2 * hidden_share],
        broad[tail : tail + chan_share],
        broad[:inner_share].T,
        broad[inner_share:tail],
    )


def solution(mesh):
    in_specs = (
        P("lat", "lon", None),
        P("lat", "lon"),
        P(),
        P(),
        P(),
        P(),
        P(),
        P(),
        P("lat", "lon", None),
    )
    out_specs = (
        P("lat", "lon", None),
        P("lat", "lon", None),
        P(None, None, ("lat", "lon")),
        P(None, ("lat", "lon")),
        P(("lat", "lon"), None),
        P(("lat", "lon"), None),
        P(None, ("lat", "lon")),
        P(("lat", "lon"), None),
    )
    return jax.shard_map(local, mesh=mesh, in_specs=in_specs, out_specs=out_specs, check_vma=False)
```
